32 devices in a mesh: groups: 2 (over y), store: 4 (over z), layer: 4 (over x, core).
Axes of the slice: x: 2, y: 2, z: 4, core: 2. Of those that a mesh axis runs over, the one named last changes fastest.
Arguments:
- query_inputs: bfloat16 [4, 256, 2, 4096], P('layer', ('groups', 'store')), parts along dimension 1, may hold values from -6 to 6
- query_grads: bfloat16 [4, 256, 2, 4096], P('layer', ('groups', 'store')), parts along dimension 1
- proj_in: bfloat16 [4, 64, 4096], P('layer')
- proj_out: bfloat16 [4, 32, 4096], P('layer'), may hold values from -0.09375 to 0.09375
- hess_inv: bfloat16 [4, 16, 128, 128], P('layer'), as said below
- store_sketch: bfloat16 [5888, 8192], P(('groups', 'store'), 'layer'), parts along dimension 0, may hold values from -6 to 6
Outputs:
- scores: bfloat16 [256, 2944], P(('groups', 'layer'), 'store'), parts along dimension 0
The draws below stay inside these ranges and needn't reach their ends.
There are 2 independent parts, one for each index of `groups`. The reference program is written for one: setup_inputs(seed, part) draws one part's arguments, and reference() takes and returns one part's arrays. A program takes and returns all parts, laid end to end along the dimension named above; an argument that names none is the same for every part. Nothing has to cross between parts.
Inputs may be any that keep to these rules, and one draw needn't show every extreme that they name: `hess_inv`: each 128 x 128 block is symmetric and positive definite.
All inputs are finite; a program needn't handle non-finite values.
Results may differ from the reference program's by a relative error of at most 0.012.
Values may be sent and summed in bfloat16 or wider, within the bound.
A program may use at most 64 MiB of HBM per device.

```python
import math
import jax
import jax.numpy as jnp
from jax import lax

D = 4096
K_IN = 64
K_OUT = 32
SKETCH = 2048
BLK = 128
BLOCKS = 16
LAYERS = 4
QUERIES = 128
TOK = 2
STORE_ROWS = 2944


def draw_query_grads(key, part):
    key = jax.random.fold_in(key, 11)
    first = jax.random.fold_in(key, 0)
    position = jnp.arange(LAYERS, dtype=jnp.float32) / max(LAYERS - 1, 1)
    values = jax.random.normal(first, (LAYERS, QUERIES, TOK, D), jnp.float32)
    growth = 3.0 ** position
    return (values * growth[:, None, None, None]).astype(jnp.bfloat16)


def draw_proj_in(key, part):
    key = jax.random.fold_in(key, 12)
    first, second = jax.random.split(key)
    values = jax.random.normal(first, (LAYERS, K_IN, D), jnp.float32)
    row_scale = jnp.exp(jax.random.uniform(second, (LAYERS, K_IN, 1), jnp.float32, math.log(0.3), math.log(3.0)))
    return (values * row_scale * D ** (-0.5)).astype(jnp.bfloat16)


def draw_hess_inv(key, part):
    key = jax.random.fold_in(key, 13)
    first, second = jax.random.split(key)
    diagonal = jax.random.uniform(first, (LAYERS, BLOCKS, BLK), jnp.float32, 1.5, 3.0)
    noise = jnp.clip(jax.random.normal(second, (LAYERS, BLOCKS, BLK, BLK), jnp.float32), -4.0, 4.0)
    mixed = (noise + jnp.swapaxes(noise, 2, 3)) * (0.5 / (2.0 * BLK) ** 0.5)
    return (mixed + diagonal[..., None] * jnp.eye(BLK, dtype=jnp.float32)).astype(jnp.bfloat16)


def steps_of(rng, extent, cuts, low, largest):
    gain, own = 1.0, jax.random.fold_in(rng, 6)
    for dim, parts in cuts:
        steps = jnp.exp(jax.random.uniform(jax.random.fold_in(own, dim), (parts,), jnp.float32, low / len(cuts), largest / len(cuts)))
        gain = gain * jnp.repeat(steps, extent[dim] // parts).reshape([-1 if axis == dim else 1 for axis in range(len(extent))])
    return gain


def gaussian(own_key, dims, width, most, cuts=(), kind=jnp.bfloat16):
    values = width * jax.random.normal(own_key, dims, jnp.float32)
    if cuts:
        values = values * steps_of(own_key, dims, cuts, -0.22, 0.18)
    return jnp.clip(values, -most, most).astype(kind)


def setup_inputs(seed: int = 0, part: int = 0) -> dict:
    seeds = jax.random.split(jax.random.key(seed), 7)
    own_keys = jax.random.split(jax.random.fold_in(seeds[6], part), 7)
    query_inputs = gaussian(own_keys[0], (LAYERS, QUERIES, TOK, D), 1.0, 6.0, ((0, 4), (1, 4)))
    query_grads = draw_query_grads(jax.random.fold_in(jax.random.fold_in(seeds[6], part), 71), part)
    proj_in = draw_proj_in(jax.random.fold_in(seeds[6], 71), part)
    proj_out = gaussian(seeds[3], (LAYERS, K_OUT, D), D ** -0.5, 0.09375, ((0, 4),))
    hess_inv = draw_hess_inv(jax.random.fold_in(seeds[6], 71), part)
    store_sketch = gaussian(own_keys[5], (STORE_ROWS, LAYERS * SKETCH), 1.0, 6.0, ((0, 4), (1, 4)))
    return {"query_inputs": query_inputs, "query_grads": query_grads, "proj_in": proj_in, "proj_out": proj_out, "hess_inv": hess_inv, "store_sketch": store_sketch}


epsilon = 1e-06

def layer_sketch(layer_args):
    inputs, gradients, project_in, project_out, inverse = layer_args
    projected_in = jnp.einsum('qtd,kd->qtk', inputs.astype(jnp.float32), project_in.astype(jnp.float32), precision=lax.Precision.HIGHEST)
    projected_out = jnp.einsum('qtd,od->qto', gradients.astype(jnp.float32), project_out.astype(jnp.float32), precision=lax.Precision.HIGHEST)
    outer_sum = jnp.einsum('qto,qtk->qok', projected_out, projected_in, precision=lax.Precision.HIGHEST)
    query_count = outer_sum.shape[0]
    blocked = outer_sum.reshape(query_count, inverse.shape[0], inverse.shape[1]).astype(jnp.bfloat16)
    precond = jnp.einsum('qbj,bij->qbi', blocked.astype(jnp.float32), inverse.astype(jnp.float32), precision=lax.Precision.HIGHEST)
    return precond.reshape(query_count, inverse.shape[0] * inverse.shape[1])

def reference(query_inputs, query_grads, proj_in, proj_out, hess_inv, store_sketch):
    precond = lax.map(layer_sketch, (query_inputs, query_grads, proj_in, proj_out, hess_inv))
    total_squares = lax.optimization_barrier(jnp.sum(precond * precond, axis=(0, 2)))
    normed = (precond * lax.rsqrt(total_squares + epsilon)[None, :, None]).astype(jnp.bfloat16)
    layers, query_count, sketch = normed.shape
    flattened = jnp.transpose(normed, (1, 0, 2)).reshape(query_count, layers * sketch)
    scores = lax.dot_general(flattened, store_sketch, (((1,), (1,)), ((), ())), preferred_element_type=jnp.float32)
    return scores.astype(jnp.bfloat16)
```

```python
import functools

import jax
import jax.numpy as jnp
from jax import lax
from jax.experimental import pallas as pl
from jax.experimental.pallas import tpu as pltpu
from jax.sharding import PartitionSpec as P

epsilon = 1e-06
MESH = pl.DeviceIdType.MESH
CHUNK = 256
LANES = 128
f32, bf16 = jnp.float32, jnp.bfloat16


def contract(a, b):
    return lax.dot_general(a, b, (((1,), (1,)), ((), ())), preferred_element_type=f32)


def repeat(count, body):
    if count == 1:
        body(0)
    else:
        lax.fori_loop(0, count, lambda i, _: (body(i), None)[1], None)


def kernel(
    stores, layers, peers_per_step,
    qin_hbm, qgr_hbm, pin_hbm, pout_hbm, hess_hbm, store_hbm, out_ref,
    qin, qgr, pin, pout, hess, store, mixed, factors, expand, unit, norms, part, got,
    load_sem, fsend_sem, frecv_sem, psend_sem, precv_sem,
):
    my_store, my_layer = lax.axis_index("store"), lax.axis_index("layer")
    queries, tokens, _ = qin.shape
    k_in, k_out = pin.shape[0], pout.shape[0]
    blocks, blk, _ = hess.shape
    rows = store_hbm.shape[0]
    chunks = part.shape[0]
    own = got.shape[2]
    tail = rows - (chunks - 1) * CHUNK

    def load(source, target, index):
        copy = pltpu.make_async_copy(source, target, load_sem.at[index])
        copy.start()
        return copy

    loads = [
        load(qin_hbm.at[0], qin, 0),
        load(pin_hbm.at[0], pin, 1),
        load(qgr_hbm.at[0], qgr, 2),
        load(pout_hbm.at[0], pout, 3),
        load(hess_hbm.at[0], hess, 4),
    ]
    store_loads = []
    for c in range(chunks):
        size = CHUNK if c < chunks - 1 else tail
        at = pl.ds(c * CHUNK, size)
        store_loads.append(load(store_hbm.at[at], store.at[at], 5 + c))

    barrier = pltpu.get_barrier_semaphore()
    for hop in range(1, stores):
        pl.semaphore_signal(
            barrier, inc=1, device_id={"store": lax.rem(my_store + hop, stores)}, device_id_type=MESH
        )
    for hop in range(1, layers):
        pl.semaphore_signal(
            barrier, inc=1, device_id={"layer": lax.rem(my_layer + hop, layers)}, device_id_type=MESH
        )

    depth = expand.shape[0]
    sketch = blocks * blk
    row = lax.rem(lax.broadcasted_iota(jnp.int32, (depth, LANES), 0), LANES)
    col = lax.broadcasted_iota(jnp.int32, (depth, LANES), 1)
    per_block = blk // k_in
    for b in range(blocks):
        hit = row == k_in + b * per_block + col // k_in
        expand[:, b * blk : (b + 1) * blk] = jnp.where(hit, 1.0, 0.0).astype(bf16)
    expand[:, sketch:] = jnp.where(row == lax.rem(col, k_in), 1.0, 0.0).astype(bf16)
    store[rows:, :] = jnp.zeros((chunks * CHUNK - rows, store.shape[1]), bf16)
    mixed[...] = jnp.zeros_like(mixed)

    loads[0].wait()
    loads[1].wait()
    mixed[:, 0:k_in] = contract(qin[...].reshape(queries * tokens, -1), pin[...])
    loads[2].wait()
    loads[3].wait()
    mixed[:, k_in : k_in + k_out] = contract(qgr[...].reshape(queries * tokens, -1), pout[...])
    for t in range(tokens):
        value = mixed[pl.ds(t, queries, stride=tokens), :]
        high = value.astype(bf16)
        factors[my_store, t * queries : (t + 1) * queries, 0:LANES] = high
        factors[my_store, t * queries : (t + 1) * queries, LANES:] = (
            value - high.astype(f32)
        ).astype(bf16)

    pl.semaphore_wait(barrier, stores + layers - 2)

    def factor_copy(hop):
        return pltpu.make_async_remote_copy(
            src_ref=factors.at[my_store],
            dst_ref=factors.at[my_store],
            send_sem=fsend_sem.at[hop - 1],
            recv_sem=frecv_sem.at[hop - 1],
            device_id={"store": lax.rem(my_store + hop, stores)},
            device_id_type=MESH,
        )

    def factor_arrival(hop):
        source = lax.rem(my_store - hop + stores, stores)
        return pltpu.make_async_remote_copy(
            src_ref=factors.at[source],
            dst_ref=factors.at[source],
            send_sem=fsend_sem.at[hop - 1],
            recv_sem=frecv_sem.at[hop - 1],
            device_id={"store": source},
            device_id_type=MESH,
        )

    for hop in range(1, stores):
        factor_copy(hop).start()
    loads[4].wait()
    for hop in range(1, stores):
        factor_arrival(hop).wait_recv()

    step_rows = peers_per_step * queries
    steps = stores // peers_per_step

    def precondition(step):
        at = pl.ds(step * peers_per_step, peers_per_step)
        joined = factors[at].reshape(peers_per_step * tokens * queries, depth)

        def spread(first):
            value = jnp.dot(joined, expand[:, first : first + blk], preferred_element_type=f32)
            return value.reshape(peers_per_step, tokens, queries, blk)

        features = spread(sketch)
        total = jnp.zeros((step_rows, blk), f32)
        to = pl.ds(pl.multiple_of(step * step_rows, step_rows), step_rows)
        for b in range(blocks):
            outer = jnp.sum(spread(b * blk) * features, axis=1)
            outer = outer.reshape(step_rows, blk).astype(bf16)
            precond = contract(outer, hess[b])
            total += precond * precond
            unit[to, b * blk : (b + 1) * blk] = precond.astype(bf16)
        norms[to, :] = jnp.broadcast_to(jnp.sum(total, axis=1, keepdims=True), (step_rows, LANES)) * 0.25

    repeat(steps, precondition)

    def part_copy(c, hop):
        peer = lax.rem(my_layer + hop, layers)
        return pltpu.make_async_remote_copy(
            src_ref=part.at[c, pl.ds(pl.multiple_of(peer * own, own), own)],
            dst_ref=got.at[c, hop - 1],
            send_sem=psend_sem.at[c, hop - 1],
            recv_sem=precv_sem.at[c, hop - 1],
            device_id={"layer": peer},
            device_id_type=MESH,
        )

    lane = lax.broadcasted_iota(jnp.int32, (step_rows, CHUNK), 1)
    for c in range(chunks):
        store_loads[c].wait()

        def score(step, c=c):
            to = pl.ds(pl.multiple_of(step * step_rows, step_rows), step_rows)
            value = contract(unit[to, :], store[c * CHUNK : (c + 1) * CHUNK, :])
            if c == chunks - 1:
                norm = norms[to, 0:1]
                high = norm.astype(bf16).astype(f32)
                value = jnp.where(lane == tail, high, value)
                value = jnp.where(lane == tail + 1, norm - high, value)
            part[c, to, :] = value.astype(bf16)

        repeat(steps, score)
        for hop in range(1, layers):
            part_copy(c, hop).start()

    mine = pl.ds(pl.multiple_of(my_layer * own, own), own)
    sums = []
    for c in range(chunks):
        value = part[c, mine, :].astype(f32)
        for hop in range(1, layers):
            part_copy(c, hop).wait_recv()
            value += got[c, hop - 1].astype(f32)
        sums.append(value)
    square = (sums[-1][:, tail : tail + 1] + sums[-1][:, tail + 1 : tail + 2]) * 4.0
    scale = lax.rsqrt(square + epsilon)
    for c in range(chunks):
        size = CHUNK if c < chunks - 1 else tail
        value = jnp.where(scale > 0.0, sums[c] * scale, 0.0).astype(bf16)
        out_ref[:, c * CHUNK : c * CHUNK + size] = value[:, :size]

    for hop in range(1, stores):
        factor_copy(hop).wait_send()
    for c in range(chunks):
        for hop in range(1, layers):
            part_copy(c, hop).wait_send()


def shards(stores, layers, query_inputs, query_grads, proj_in, proj_out, hess_inv, store_sketch):
    _, queries, tokens, width = query_inputs.shape
    k_in, k_out = proj_in.shape[1], proj_out.shape[1]
    _, blocks, blk, _ = hess_inv.shape
    rows, sketch = store_sketch.shape
    chunks = -(-(rows + 2) // CHUNK)
    every = queries * stores
    own = every // layers
    peers_per_step = 4 if stores % 4 == 0 else 1
    scratch = [
        pltpu.VMEM((queries, tokens, width), bf16),
        pltpu.VMEM((queries, tokens, width), bf16),
        pltpu.VMEM((k_in, width), bf16),
        pltpu.VMEM((k_out, width), bf16),
        pltpu.VMEM((blocks, blk, blk), bf16),
        pltpu.VMEM((chunks * CHUNK, sketch), bf16),
        pltpu.VMEM((tokens * queries, LANES), f32),
        pltpu.VMEM((stores, tokens * queries, 2 * LANES), bf16),
        pltpu.VMEM((2 * LANES, sketch + blk), bf16),
        pltpu.VMEM((every, sketch), bf16),
        pltpu.VMEM((every, LANES), f32),
        pltpu.VMEM((chunks, every, CHUNK), bf16),
        pltpu.VMEM((chunks, layers - 1, own, CHUNK), bf16),
        pltpu.SemaphoreType.DMA((5 + chunks,)),
        pltpu.SemaphoreType.DMA((stores - 1,)),
        pltpu.SemaphoreType.DMA((stores - 1,)),
        pltpu.SemaphoreType.DMA((chunks, layers - 1)),
        pltpu.SemaphoreType.DMA((chunks, layers - 1)),
    ]
    return pl.pallas_call(
        functools.partial(kernel, stores, layers, peers_per_step),
        out_shape=jax.ShapeDtypeStruct((own, rows), bf16),
        in_specs=[pl.BlockSpec(memory_space=pl.ANY)] * 6,
        out_specs=pl.BlockSpec(memory_space=pltpu.VMEM),
        scratch_shapes=scratch,
        compiler_params=pltpu.CompilerParams(
            collective_id=0, has_side_effects=True, vmem_limit_bytes=48 * 2**20
        ),
    )(query_inputs, query_grads, proj_in, proj_out, hess_inv, store_sketch)


def solution(mesh):
    return jax.shard_map(
        functools.partial(shards, mesh.shape["store"], mesh.shape["layer"]),
        mesh=mesh,
        in_specs=(
            P("layer", ("groups", "store"), None, None),
            P("layer", ("groups", "store"), None, None),
            P("layer", None, None),
            P("layer", None, None),
            P("layer", None, None, None),
            P(("groups", "store"), "layer"),
        ),
        out_specs=P(("groups", "layer"), "store"),
        check_vma=False,
    )
```

```python
import functools

import jax
import jax.numpy as jnp
from jax import lax
from jax.experimental import pallas as pl
from jax.experimental.pallas import tpu as pltpu
from jax.sharding import PartitionSpec as P

epsilon = 1e-06
MESH = pl.DeviceIdType.MESH
CHUNK = 256
LANES = 128
f32, bf16 = jnp.float32, jnp.bfloat16


def contract(a, b):
    return lax.dot_general(a, b, (((1,), (1,)), ((), ())), preferred_element_type=f32)


def repeat(count, body):
    if count == 1:
        body(0)
    else:
        lax.fori_loop(0, count, lambda i, _: (body(i), None)[1], None)


def kernel(
    stores, layers, peers_per_step,
    qin_hbm, qgr_hbm, pin_hbm, pout_hbm, hess_hbm, store_hbm, out_ref,
    qin, qgr, pin, pout, hess, store, mixed, factors, expand, unit, norms, part, got,
    load_sem, fsend_sem, frecv_sem, psend_sem, precv_sem,
):
    my_store, my_layer = lax.axis_index("store"), lax.axis_index("layer")
    queries, tokens, _ = qin.shape
    k_in, k_out = pin.shape[0], pout.shape[0]
    blocks, blk, _ = hess.shape
    rows = store_hbm.shape[0]
    chunks = part.shape[0]
    own = got.shape[2]
    tail = rows - (chunks - 1) * CHUNK

    def load(source, target, index):
        copy = pltpu.make_async_copy(source, target, load_sem.at[index])
        copy.start()
        return copy

    loads = [
        load(qin_hbm.at[0], qin, 0),
        load(pin_hbm.at[0], pin, 1),
        load(qgr_hbm.at[0], qgr, 2),
        load(pout_hbm.at[0], pout, 3),
        load(hess_hbm.at[0], hess, 4),
    ]
    store_loads = []
    for c in range(chunks):
        size = CHUNK if c < chunks - 1 else tail
        at = pl.ds(c * CHUNK, size)
        store_loads.append(load(store_hbm.at[at], store.at[at], 5 + c))

    barrier = pltpu.get_barrier_semaphore()
    for hop in range(1, stores):
        pl.semaphore_signal(
            barrier, inc=1, device_id={"store": lax.rem(my_store + hop, stores)}, device_id_type=MESH
        )
    for hop in range(1, layers):
        pl.semaphore_signal(
            barrier, inc=1, device_id={"layer": lax.rem(my_layer + hop, layers)}, device_id_type=MESH
        )

    depth = expand.shape[0]
    sketch = blocks * blk
    row = lax.rem(lax.broadcasted_iota(jnp.int32, (depth, LANES), 0), LANES)
    col = lax.broadcasted_iota(jnp.int32, (depth, LANES), 1)
    per_block = blk // k_in
    for b in range(blocks):
        hit = row == k_in + b * per_block + col // k_in
        expand[:, b * blk : (b + 1) * blk] = jnp.where(hit, 1.0, 0.0).astype(bf16)
    expand[:, sketch:] = jnp.where(row == lax.rem(col, k_in), 1.0, 0.0).astype(bf16)
    store[rows:, :] = jnp.zeros((chunks * CHUNK - rows, store.shape[1]), bf16)
    mixed[...] = jnp.zeros_like(mixed)

    loads[0].wait()
    loads[1].wait()
    mixed[:, 0:k_in] = contract(qin[...].reshape(queries * tokens, -1), pin[...])
    loads[2].wait()
    loads[3].wait()
    mixed[:, k_in : k_in + k_out] = contract(qgr[...].reshape(queries * tokens, -1), pout[...])
    for t in range(tokens):
        value = mixed[pl.ds(t, queries, stride=tokens), :]
        high = value.astype(bf16)
        factors[my_store, t * queries : (t + 1) * queries, 0:LANES] = high
        factors[my_store, t * queries : (t + 1) * queries, LANES:] = (
            value - high.astype(f32)
        ).astype(bf16)

    pl.semaphore_wait(barrier, stores + layers - 2)

    def factor_copy(hop):
        return pltpu.make_async_remote_copy(
            src_ref=factors.at[my_store],
            dst_ref=factors.at[my_store],
            send_sem=fsend_sem.at[hop - 1],
            recv_sem=frecv_sem.at[hop - 1],
            device_id={"store": lax.rem(my_store + hop, stores)},
            device_id_type=MESH,
        )

    def factor_arrival(hop):
        source = lax.rem(my_store - hop + stores, stores)
        return pltpu.make_async_remote_copy(
            src_ref=factors.at[source],
            dst_ref=factors.at[source],
            send_sem=fsend_sem.at[hop - 1],
            recv_sem=frecv_sem.at[hop - 1],
            device_id={"store": source},
            device_id_type=MESH,
        )

    for hop in range(1, stores):
        factor_copy(hop).start()
    loads[4].wait()
    for hop in range(1, stores):
        factor_arrival(hop).wait_recv()

    step_rows = peers_per_step * queries
    steps = stores // peers_per_step

    def precondition(step):
        at = pl.ds(step * peers_per_step, peers_per_step)
        joined = factors[at].reshape(peers_per_step * tokens * queries, depth)

        def spread(first):
            value = jnp.dot(joined, expand[:, first : first + blk], preferred_element_type=f32)
            return value.reshape(peers_per_step, tokens, queries, blk)

        features = spread(sketch)
        total = jnp.zeros((step_rows, blk), f32)
        to = pl.ds(pl.multiple_of(step * step_rows, step_rows), step_rows)
        for b in range(blocks):
            outer = jnp.sum(spread(b * blk) * features, axis=1)
            outer = outer.reshape(step_rows, blk).astype(bf16)
            precond = contract(outer, hess[b])
            total += precond * precond
            unit[to, b * blk : (b + 1) * blk] = precond.astype(bf16)
        norms[to, :] = jnp.broadcast_to(jnp.sum(total, axis=1, keepdims=True), (step_rows, LANES)) * 0.25

    repeat(steps, precondition)

    def part_copy(c, hop):
        peer = lax.rem(my_layer + hop, layers)
        return pltpu.make_async_remote_copy(
            src_ref=part.at[c, pl.ds(pl.multiple_of(peer * own, own), own)],
            dst_ref=got.at[c, hop - 1],
            send_sem=psend_sem.at[c, hop - 1],
            recv_sem=precv_sem.at[c, hop - 1],
            device_id={"layer": peer},
            device_id_type=MESH,
        )

    lane = lax.broadcasted_iota(jnp.int32, (step_rows, CHUNK), 1)
    for c in range(chunks):
        store_loads[c].wait()

        def score(step, c=c):
            to = pl.ds(pl.multiple_of(step * step_rows, step_rows), step_rows)
            value = contract(unit[to, :], store[c * CHUNK : (c + 1) * CHUNK, :])
            if c == chunks - 1:
                norm = norms[to, 0:1]
                high = norm.astype(bf16).astype(f32)
                value = jnp.where(lane == tail, high, value)
                value = jnp.where(lane == tail + 1, norm - high, value)
            part[c, to, :] = value.astype(bf16)

        repeat(steps, score)
        for hop in range(1, layers):
            part_copy(c, hop).start()

    mine = pl.ds(pl.multiple_of(my_layer * own, own), own)
    sums = []
    for c in range(chunks):
        value = part[c, mine, :].astype(f32)
        for hop in range(1, layers):
            part_copy(c, hop).wait_recv()
            value += got[c, hop - 1].astype(f32)
        sums.append(value)
    square = (sums[-1][:, tail : tail + 1] + sums[-1][:, tail + 1 : tail + 2]) * 4.0
    scale = lax.rsqrt(square + epsilon)
    for c in range(chunks):
        size = CHUNK if c < chunks - 1 else tail
        value = jnp.where(scale > 0.0, sums[c] * scale, 0.0).astype(bf16)
        out_ref[:, c * CHUNK : c * CHUNK + size] = value[:, :size]

    for hop in range(1, stores):
        factor_copy(hop).wait_send()
    for c in range(chunks):
        for hop in range(1, layers):
            part_copy(c, hop).wait_send()


def shards(stores, layers, query_inputs, query_grads, proj_in, proj_out, hess_inv, store_sketch):
    _, queries, tokens, width = query_inputs.shape
    k_in, k_out = proj_in.shape[1], proj_out.shape[1]
    _, blocks, blk, _ = hess_inv.shape
    rows, sketch = store_sketch.shape
    chunks = -(-(rows + 2) // CHUNK)
    every = queries * stores
    own = every // layers
    peers_per_step = 4 if stores % 4 == 0 else 1
    scratch = [
        pltpu.VMEM((queries, tokens, width), bf16),
        pltpu.VMEM((queries, tokens, width), bf16),
        pltpu.VMEM((k_in, width), bf16),
        pltpu.VMEM((k_out, width), bf16),
        pltpu.VMEM((blocks, blk, blk), bf16),
        pltpu.VMEM((chunks * CHUNK, sketch), bf16),
        pltpu.VMEM((tokens * queries, LANES), f32),
        pltpu.VMEM((stores, tokens * queries, 2 * LANES), bf16),
        pltpu.VMEM((2 * LANES, sketch + blk), bf16),
        pltpu.VMEM((every, sketch), bf16),
        pltpu.VMEM((every, LANES), f32),
        pltpu.VMEM((chunks, every, CHUNK), bf16),
        pltpu.VMEM((chunks, layers - 1, own, CHUNK), bf16),
        pltpu.SemaphoreType.DMA((5 + chunks,)),
        pltpu.SemaphoreType.DMA((stores - 1,)),
        pltpu.SemaphoreType.DMA((stores - 1,)),
        pltpu.SemaphoreType.DMA((chunks, layers - 1)),
        pltpu.SemaphoreType.DMA((chunks, layers - 1)),
    ]
    return pl.pallas_call(
        functools.partial(kernel, stores, layers, peers_per_step),
        out_shape=jax.ShapeDtypeStruct((own, rows), bf16),
        in_specs=[pl.BlockSpec(memory_space=pltpu.HBM)] * 6,
        out_specs=pl.BlockSpec(memory_space=pltpu.VMEM),
        scratch_shapes=scratch,
        compiler_params=pltpu.CompilerParams(
            collective_id=0, has_side_effects=True, vmem_limit_bytes=64 * 2**20 - 2**17
        ),
    )(query_inputs, query_grads, proj_in, proj_out, hess_inv, store_sketch)


def solution(mesh):
    return jax.shard_map(
        functools.partial(shards, mesh.shape["store"], mesh.shape["layer"]),
        mesh=mesh,
        in_specs=(
            P("layer", ("groups", "store"), None, None),
            P("layer", ("groups", "store"), None, None),
            P("layer", None, None),
            P("layer", None, None),
            P("layer", None, None, None),
            P(("groups", "store"), "layer"),
        ),
        out_specs=P(("groups", "layer"), "store"),
        check_vma=False,
    )
```

```python
import functools

import jax
import jax.numpy as jnp
from jax import lax
from jax.experimental import pallas as pl
from jax.experimental.pallas import tpu as pltpu
from jax.sharding import PartitionSpec as P

epsilon = 1e-06
MESH = pl.DeviceIdType.MESH
CHUNK = 256
GROUP = 3
LANES = 128
f32, bf16 = jnp.float32, jnp.bfloat16


def contract(a, b):
    return lax.dot_general(a, b, (((1,), (1,)), ((), ())), preferred_element_type=f32)


def repeat(count, body):
    if count == 1:
        body(0)
    else:
        lax.fori_loop(0, count, lambda i, _: (body(i), None)[1], None)


def kernel(
    stores, layers, group,
    qin_hbm, qgr_hbm, pin_hbm, pout_hbm, hess_hbm, store_hbm, out_ref,
    qin, qgr, pin, pout, hess, store, mixed, factors, expand, unit, norms, part, got,
    load_sem, fsend_sem, frecv_sem, psend_sem, precv_sem,
):
    my_store, my_layer = lax.axis_index("store"), lax.axis_index("layer")
    queries, tokens, _ = qin.shape
    k_in, k_out = pin.shape[0], pout.shape[0]
    blocks, blk, _ = hess.shape
    rows = store_hbm.shape[0]
    chunks = part.shape[0]
    own = got.shape[2]
    tail = rows - (chunks - 1) * CHUNK

    def load(source, target, index):
        copy = pltpu.make_async_copy(source, target, load_sem.at[index])
        copy.start()
        return copy

    loads = [
        load(qin_hbm.at[0], qin, 0),
        load(pin_hbm.at[0], pin, 1),
        load(qgr_hbm.at[0], qgr, 2),
        load(pout_hbm.at[0], pout, 3),
        load(hess_hbm.at[0], hess, 4),
    ]
    store_loads = []
    for c in range(chunks):
        size = CHUNK if c < chunks - 1 else tail
        at = pl.ds(c * CHUNK, size)
        store_loads.append(load(store_hbm.at[at], store.at[at], 5 + c))

    barrier = pltpu.get_barrier_semaphore()
    for hop in range(1, stores):
        pl.semaphore_signal(
            barrier, inc=1, device_id={"store": lax.rem(my_store + hop, stores)}, device_id_type=MESH
        )
    for hop in range(1, layers):
        pl.semaphore_signal(
            barrier, inc=1, device_id={"layer": lax.rem(my_layer + hop, layers)}, device_id_type=MESH
        )

    depth = expand.shape[0]
    sketch = blocks * blk
    row = lax.rem(lax.broadcasted_iota(jnp.int32, (depth, LANES), 0), LANES)
    col = lax.broadcasted_iota(jnp.int32, (depth, LANES), 1)
    per_block = blk // k_in
    pair = 2 if blocks % 2 == 0 else 1
    step_rows = min(LANES, unit.shape[0])
    steps = unit.shape[0] // step_rows
    for b in range(blocks):
        hit = row == k_in + b * per_block + col // k_in
        expand[:, b * blk : (b + 1) * blk] = jnp.where(hit, 1.0, 0.0).astype(bf16)
    expand[:, sketch:] = jnp.where(row == lax.rem(col, k_in), 1.0, 0.0).astype(bf16)
    store[rows:, :] = jnp.zeros((chunks * CHUNK - rows, store.shape[1]), bf16)
    mixed[...] = jnp.zeros_like(mixed)

    loads[0].wait()
    loads[1].wait()
    mixed[:, 0:k_in] = contract(qin[...].reshape(queries * tokens, -1), pin[...])
    loads[2].wait()
    loads[3].wait()
    mixed[:, k_in : k_in + k_out] = contract(qgr[...].reshape(queries * tokens, -1), pout[...])
    for t in range(tokens):
        value = mixed[pl.ds(t, queries, stride=tokens), :]
        high = value.astype(bf16)
        factors[my_store, t * queries : (t + 1) * queries, 0:LANES] = high
        factors[my_store, t * queries : (t + 1) * queries, LANES:] = (
            value - high.astype(f32)
        ).astype(bf16)

    pl.semaphore_wait(barrier, stores + layers - 2)

    def factor_copy(hop):
        return pltpu.make_async_remote_copy(
            src_ref=factors.at[my_store],
            dst_ref=factors.at[my_store],
            send_sem=fsend_sem.at[hop - 1],
            recv_sem=frecv_sem.at[my_store],
            device_id={"store": lax.rem(my_store + hop, stores)},
            device_id_type=MESH,
        )

    def nearest(k):
        up = k + (my_store <= k).astype(jnp.int32)
        down = stores - 1 - k
        down = down - (down <= my_store).astype(jnp.int32)
        return jnp.where(2 * my_store < stores, up, down)

    def await_factors(source):
        pltpu.make_async_remote_copy(
            src_ref=factors.at[source],
            dst_ref=factors.at[source],
            send_sem=fsend_sem.at[0],
            recv_sem=frecv_sem.at[source],
            device_id={"store": source},
            device_id_type=MESH,
        ).wait_recv()

    def precondition(sources):
        count = len(sources)
        joined = [factors[source] for source in sources]
        joined = joined[0] if count == 1 else jnp.concatenate(joined, axis=0)

        def spread(first, size):
            value = jnp.dot(joined, expand[:, first : first + size], preferred_element_type=f32)
            return value.reshape(count, tokens, queries, size)

        features = spread(sketch, blk)
        total = jnp.zeros((count * queries, blk), f32)
        for b in range(0, blocks, pair):
            wide = spread(b * blk, pair * blk)
            for i in range(pair):
                outer = jnp.sum(wide[..., i * blk : (i + 1) * blk] * features, axis=1)
                outer = outer.reshape(count * queries, blk).astype(bf16)
                precond = contract(outer, hess[b + i])
                total += precond * precond
                precond = precond.astype(bf16)
                for n, source in enumerate(sources):
                    to = pl.ds(pl.multiple_of(source * queries, queries), queries)
                    unit[to, (b + i) * blk : (b + i + 1) * blk] = precond[n * queries : (n + 1) * queries]
        square = jnp.broadcast_to(jnp.sum(total, axis=1, keepdims=True), total.shape) * 0.25
        for n, source in enumerate(sources):
            to = pl.ds(pl.multiple_of(source * queries, queries), queries)
            norms[to, :] = square[n * queries : (n + 1) * queries]

    for hop in range(stores - 1, 0, -1):
        factor_copy(hop).start()
    loads[4].wait()
    precondition([my_store])

    def arrived(step):
        sources = [nearest(step * group + k) for k in range(group)]
        for source in sources:
            await_factors(source)
        precondition(sources)

    if stores - 1 <= 4:
        for step in range((stores - 1) // group):
            arrived(step)
    else:
        repeat((stores - 1) // group, arrived)

    def part_copy(c, hop):
        peer = lax.rem(my_layer + hop, layers)
        return pltpu.make_async_remote_copy(
            src_ref=part.at[c, pl.ds(pl.multiple_of(peer * own, own), own)],
            dst_ref=got.at[c, hop - 1],
            send_sem=psend_sem.at[c, hop - 1],
            recv_sem=precv_sem.at[c, hop - 1],
            device_id={"layer": peer},
            device_id_type=MESH,
        )

    lane = lax.broadcasted_iota(jnp.int32, (step_rows, CHUNK), 1)
    for c in range(chunks):
        store_loads[c].wait()

        def score(step, c=c):
            to = pl.ds(pl.multiple_of(step * step_rows, step_rows), step_rows)
            value = contract(unit[to, :], store[c * CHUNK : (c + 1) * CHUNK, :])
            if c == chunks - 1:
                norm = norms[to, 0:1]
                high = norm.astype(bf16).astype(f32)
                value = jnp.where(lane == tail, high, value)
                value = jnp.where(lane == tail + 1, norm - high, value)
            part[c, to, :] = value.astype(bf16)

        repeat(steps, score)
        for hop in range(1, layers):
            part_copy(c, hop).start()

    mine = pl.ds(pl.multiple_of(my_layer * own, own), own)
    sums = []
    for c in range(chunks):
        value = part[c, mine, :].astype(f32)
        for hop in range(1, layers):
            part_copy(c, hop).wait_recv()
            value += got[c, hop - 1].astype(f32)
        sums.append(value)
    square = (sums[-1][:, tail : tail + 1] + sums[-1][:, tail + 1 : tail + 2]) * 4.0
    scale = lax.rsqrt(square + epsilon)
    for c in range(chunks):
        size = CHUNK if c < chunks - 1 else tail
        value = jnp.where(scale > 0.0, sums[c] * scale, 0.0).astype(bf16)
        out_ref[:, c * CHUNK : c * CHUNK + size] = value[:, :size]

    for hop in range(1, stores):
        factor_copy(hop).wait_send()
    for c in range(chunks):
        for hop in range(1, layers):
            part_copy(c, hop).wait_send()


def shards(stores, layers, query_inputs, query_grads, proj_in, proj_out, hess_inv, store_sketch):
    _, queries, tokens, width = query_inputs.shape
    k_in, k_out = proj_in.shape[1], proj_out.shape[1]
    _, blocks, blk, _ = hess_inv.shape
    rows, sketch = store_sketch.shape
    chunks = -(-(rows + 2) // CHUNK)
    every = queries * stores
    own = every // layers
    group = GROUP if (stores - 1) % GROUP == 0 else 1
    scratch = [
        pltpu.VMEM((queries, tokens, width), bf16),
        pltpu.VMEM((queries, tokens, width), bf16),
        pltpu.VMEM((k_in, width), bf16),
        pltpu.VMEM((k_out, width), bf16),
        pltpu.VMEM((blocks, blk, blk), bf16),
        pltpu.VMEM((chunks * CHUNK, sketch), bf16),
        pltpu.VMEM((tokens * queries, LANES), f32),
        pltpu.VMEM((stores, tokens * queries, 2 * LANES), bf16),
        pltpu.VMEM((2 * LANES, sketch + blk), bf16),
        pltpu.VMEM((every, sketch), bf16),
        pltpu.VMEM((every, LANES), f32),
        pltpu.VMEM((chunks, every, CHUNK), bf16),
        pltpu.VMEM((chunks, layers - 1, own, CHUNK), bf16),
        pltpu.SemaphoreType.DMA((5 + chunks,)),
        pltpu.SemaphoreType.DMA((stores - 1,)),
        pltpu.SemaphoreType.DMA((stores,)),
        pltpu.SemaphoreType.DMA((chunks, layers - 1)),
        pltpu.SemaphoreType.DMA((chunks, layers - 1)),
    ]
    return pl.pallas_call(
        functools.partial(kernel, stores, layers, group),
        out_shape=pltpu.VMEM((own, rows), bf16),
        in_specs=[pl.BlockSpec(memory_space=pltpu.HBM)] * 6,
        out_specs=pl.BlockSpec(memory_space=pltpu.VMEM),
        scratch_shapes=scratch,
        compiler_params=pltpu.CompilerParams(
            collective_id=0, has_side_effects=True, vmem_limit_bytes=48 * 2**20
        ),
    )(
        *(
            pltpu.with_memory_space_constraint(x, pltpu.HBM)
            for x in (query_inputs, query_grads, proj_in, proj_out, hess_inv, store_sketch)
        )
    )


def solution(mesh):
    return jax.shard_map(
        functools.partial(shards, mesh.shape["store"], mesh.shape["layer"]),
        mesh=mesh,
        in_specs=(
            P("layer", ("groups", "store"), None, None),
            P("layer", ("groups", "store"), None, None),
            P("layer", None, None),
            P("layer", None, None),
            P("layer", None, None, None),
            P(("groups", "store"), "layer"),
        ),
        out_specs=P(("groups", "layer"), "store"),
        check_vma=False,
    )
```

```python
import functools

import jax
import jax.numpy as jnp
from jax import lax
from jax.experimental import pallas as pl
from jax.experimental.pallas import tpu as pltpu
from jax.sharding import PartitionSpec as P

epsilon = 1e-06
MESH = pl.DeviceIdType.MESH
CHUNK = 384
GROUP = 3
LANES = 128
f32, bf16 = jnp.float32, jnp.bfloat16


def contract(a, b):
    return lax.dot_general(a, b, (((1,), (1,)), ((), ())), preferred_element_type=f32)


def repeat(count, body):
    if count == 1:
        body(0)
    else:
        lax.fori_loop(0, count, lambda i, _: (body(i), None)[1], None)


def kernel(
    stores, layers, group,
    qin_hbm, qgr_hbm, pin_hbm, pout_hbm, hess_hbm, store_hbm, out_ref,
    qin, qgr, pin, pout, hess, store, mixed, factors, expand, unit, norms, part, got,
    load_sem, fsend_sem, frecv_sem, psend_sem, precv_sem,
):
    my_store, my_layer = lax.axis_index("store"), lax.axis_index("layer")
    queries, tokens, _ = qin.shape
    k_in, k_out = pin.shape[0], pout.shape[0]
    blocks, blk, _ = hess.shape
    rows = store_hbm.shape[0]
    chunks = part.shape[0]
    own = got.shape[2]
    tail = rows - (chunks - 1) * CHUNK

    def load(source, target, index):
        copy = pltpu.make_async_copy(source, target, load_sem.at[index])
        copy.start()
        return copy

    loads = [
        load(qin_hbm.at[0], qin, 0),
        load(pin_hbm.at[0], pin, 1),
        load(qgr_hbm.at[0], qgr, 2),
        load(pout_hbm.at[0], pout, 3),
        load(hess_hbm.at[0], hess, 4),
    ]
    store_loads = []
    for c in range(chunks):
        size = CHUNK if c < chunks - 1 else tail
        at = pl.ds(c * CHUNK, size)
        store_loads.append(load(store_hbm.at[at], store.at[at], 5 + c))

    barrier = pltpu.get_barrier_semaphore()
    for hop in range(1, stores):
        pl.semaphore_signal(
            barrier, inc=1, device_id={"store": lax.rem(my_store + hop, stores)}, device_id_type=MESH
        )
    for hop in range(1, layers):
        pl.semaphore_signal(
            barrier, inc=1, device_id={"layer": lax.rem(my_layer + hop, layers)}, device_id_type=MESH
        )

    depth = expand.shape[0]
    sketch = blocks * blk
    row = lax.rem(lax.broadcasted_iota(jnp.int32, (depth, LANES), 0), LANES)
    col = lax.broadcasted_iota(jnp.int32, (depth, LANES), 1)
    per_block = blk // k_in
    pair = 2 if blocks % 2 == 0 else 1
    step_rows = min(LANES, unit.shape[0])
    steps = unit.shape[0] // step_rows
    for b in range(blocks):
        hit = row == k_in + b * per_block + col // k_in
        expand[:, b * blk : (b + 1) * blk] = jnp.where(hit, 1.0, 0.0).astype(bf16)
    expand[:, sketch:] = jnp.where(row == lax.rem(col, k_in), 1.0, 0.0).astype(bf16)
    store[rows:, :] = jnp.zeros((chunks * CHUNK - rows, store.shape[1]), bf16)
    mixed[...] = jnp.zeros_like(mixed)

    loads[0].wait()
    loads[1].wait()
    mixed[:, 0:k_in] = contract(qin[...].reshape(queries * tokens, -1), pin[...])
    loads[2].wait()
    loads[3].wait()
    mixed[:, k_in : k_in + k_out] = contract(qgr[...].reshape(queries * tokens, -1), pout[...])
    for t in range(tokens):
        value = mixed[pl.ds(t, queries, stride=tokens), :]
        high = value.astype(bf16)
        factors[my_store, t * queries : (t + 1) * queries, 0:LANES] = high

    pl.semaphore_wait(barrier, stores + layers - 2)

    def factor_copy(hop):
        return pltpu.make_async_remote_copy(
            src_ref=factors.at[my_store],
            dst_ref=factors.at[my_store],
            send_sem=fsend_sem.at[hop - 1],
            recv_sem=frecv_sem.at[my_store],
            device_id={"store": lax.rem(my_store + hop, stores)},
            device_id_type=MESH,
        )

    def nearest(k):
        up = k + (my_store <= k).astype(jnp.int32)
        down = stores - 1 - k
        down = down - (down <= my_store).astype(jnp.int32)
        return jnp.where(2 * my_store < stores, up, down)

    def await_factors(source):
        pltpu.make_async_remote_copy(
            src_ref=factors.at[source],
            dst_ref=factors.at[source],
            send_sem=fsend_sem.at[0],
            recv_sem=frecv_sem.at[source],
            device_id={"store": source},
            device_id_type=MESH,
        ).wait_recv()

    def precondition(sources):
        count = len(sources)
        joined = [factors[source] for source in sources]
        joined = joined[0] if count == 1 else jnp.concatenate(joined, axis=0)

        def spread(first, size):
            value = jnp.dot(joined, expand[:, first : first + size], preferred_element_type=f32)
            return value.reshape(count, tokens, queries, size)

        features = spread(sketch, blk)
        total = jnp.zeros((count * queries, blk), f32)
        outers = []
        for b in range(0, blocks, pair):
            wide = spread(b * blk, pair * blk)
            for i in range(pair):
                outer = jnp.sum(wide[..., i * blk : (i + 1) * blk] * features, axis=1)
                outers.append(outer.reshape(count * queries, blk).astype(bf16))
        for b in range(blocks):
            precond = jnp.dot(outers[b], hess[b], preferred_element_type=f32)
            total += precond * precond
            precond = precond.astype(bf16)
            for n, source in enumerate(sources):
                to = pl.ds(pl.multiple_of(source * queries, queries), queries)
                unit[to, b * blk : (b + 1) * blk] = precond[n * queries : (n + 1) * queries]
        square = jnp.broadcast_to(jnp.sum(total, axis=1, keepdims=True), total.shape) * 0.25
        for n, source in enumerate(sources):
            to = pl.ds(pl.multiple_of(source * queries, queries), queries)
            norms[to, :] = square[n * queries : (n + 1) * queries]

    for hop in range(stores - 1, 0, -1):
        factor_copy(hop).start()
    loads[4].wait()
    precondition([my_store])

    def arrived(step):
        sources = [nearest(step * group + k) for k in range(group)]
        for source in sources:
            await_factors(source)
        precondition(sources)

    if stores - 1 <= 4:
        for step in range((stores - 1) // group):
            arrived(step)
    else:
        repeat((stores - 1) // group, arrived)

    def part_copy(c, hop):
        peer = lax.rem(my_layer + hop, layers)
        return pltpu.make_async_remote_copy(
            src_ref=part.at[c, pl.ds(pl.multiple_of(peer * own, own), own)],
            dst_ref=got.at[c, hop - 1],
            send_sem=psend_sem.at[c, hop - 1],
            recv_sem=precv_sem.at[c, hop - 1],
            device_id={"layer": peer},
            device_id_type=MESH,
        )

    lane = lax.broadcasted_iota(jnp.int32, (step_rows, CHUNK), 1)
    for c in range(chunks):
        store_loads[c].wait()

        def score(step, c=c):
            to = pl.ds(pl.multiple_of(step * step_rows, step_rows), step_rows)
            value = contract(unit[to, :], store[c * CHUNK : (c + 1) * CHUNK, :])
            if c == chunks - 1:
                norm = norms[to, 0:1]
                high = norm.astype(bf16).astype(f32)
                value = jnp.where(lane == tail, high, value)
                value = jnp.where(lane == tail + 1, norm - high, value)
            part[c, to, :] = value.astype(bf16)

        repeat(steps, score)
        for hop in range(1, layers):
            part_copy(c, hop).start()

    mine = pl.ds(pl.multiple_of(my_layer * own, own), own)
    sums = []
    for c in range(chunks):
        value = part[c, mine, :].astype(f32)
        for hop in range(1, layers):
            part_copy(c, hop).wait_recv()
            value += got[c, hop - 1].astype(f32)
        sums.append(value)
    square = (sums[-1][:, tail : tail + 1] + sums[-1][:, tail + 1 : tail + 2]) * 4.0
    scale = lax.rsqrt(square + epsilon)
    for c in range(chunks):
        size = CHUNK if c < chunks - 1 else tail
        value = jnp.where(scale > 0.0, sums[c] * scale, 0.0).astype(bf16)
        out_ref[:, c * CHUNK : c * CHUNK + size] = value[:, :size]

    for hop in range(1, stores):
        factor_copy(hop).wait_send()
    for c in range(chunks):
        for hop in range(1, layers):
            part_copy(c, hop).wait_send()


def shards(stores, layers, query_inputs, query_grads, proj_in, proj_out, hess_inv, store_sketch):
    _, queries, tokens, width = query_inputs.shape
    k_in, k_out = proj_in.shape[1], proj_out.shape[1]
    _, blocks, blk, _ = hess_inv.shape
    rows, sketch = store_sketch.shape
    chunks = -(-(rows + 2) // CHUNK)
    every = queries * stores
    own = every // layers
    group = GROUP if (stores - 1) % GROUP == 0 else 1
    scratch = [
        pltpu.VMEM((queries, tokens, width), bf16),
        pltpu.VMEM((queries, tokens, width), bf16),
        pltpu.VMEM((k_in, width), bf16),
        pltpu.VMEM((k_out, width), bf16),
        pltpu.VMEM((blocks, blk, blk), bf16),
        pltpu.VMEM((chunks * CHUNK, sketch), bf16),
        pltpu.VMEM((tokens * queries, LANES), f32),
        pltpu.VMEM((stores, tokens * queries, LANES), bf16),
        pltpu.VMEM((LANES, sketch + blk), bf16),
        pltpu.VMEM((every, sketch), bf16),
        pltpu.VMEM((every, LANES), f32),
        pltpu.VMEM((chunks, every, CHUNK), bf16),
        pltpu.VMEM((chunks, layers - 1, own, CHUNK), bf16),
        pltpu.SemaphoreType.DMA((5 + chunks,)),
        pltpu.SemaphoreType.DMA((stores - 1,)),
        pltpu.SemaphoreType.DMA((stores,)),
        pltpu.SemaphoreType.DMA((chunks, layers - 1)),
        pltpu.SemaphoreType.DMA((chunks, layers - 1)),
    ]
    return pl.pallas_call(
        functools.partial(kernel, stores, layers, group),
        out_shape=pltpu.VMEM((own, rows), bf16),
        in_specs=[pl.BlockSpec(memory_space=pltpu.HBM)] * 6,
        out_specs=pl.BlockSpec(memory_space=pltpu.VMEM),
        scratch_shapes=scratch,
        compiler_params=pltpu.CompilerParams(
            collective_id=0, has_side_effects=True, vmem_limit_bytes=48 * 2**20
        ),
    )(
        *(
            pltpu.with_memory_space_constraint(x, pltpu.HBM)
            for x in (query_inputs, query_grads, proj_in, proj_out, hess_inv, store_sketch)
        )
    )


def solution(mesh):
    return jax.shard_map(
        functools.partial(shards, mesh.shape["store"], mesh.shape["layer"]),
        mesh=mesh,
        in_specs=(
            P("layer", ("groups", "store"), None, None),
            P("layer", ("groups", "store"), None, None),
            P("layer", None, None),
            P("layer", None, None),
            P("layer", None, None, None),
            P(("groups", "store"), "layer"),
        ),
        out_specs=P(("groups", "layer"), "store"),
        check_vma=False,
    )
```

```python
import functools

import jax
import jax.numpy as jnp
from jax import lax
from jax.experimental import pallas as pl
from jax.experimental.pallas import tpu as pltpu
from jax.sharding import PartitionSpec as P

epsilon = 1e-06
MESH = pl.DeviceIdType.MESH
CHUNK = 384
GROUP = 1
LANES = 128
f32, bf16 = jnp.float32, jnp.bfloat16


def contract(a, b):
    return lax.dot_general(a, b, (((1,), (1,)), ((), ())), preferred_element_type=f32)


def repeat(count, body):
    if count == 1:
        body(0)
    else:
        lax.fori_loop(0, count, lambda i, _: (body(i), None)[1], None)


def kernel(
    stores, layers, group,
    qin_hbm, qgr_hbm, pin_hbm, pout_hbm, hess_hbm, store_hbm, out_ref,
    qin, qgr, pin, pout, hess, store, mixed, factors, expand, unit, norms, part, got,
    load_sem, fsend_sem, frecv_sem, psend_sem, precv_sem,
):
    my_store, my_layer = lax.axis_index("store"), lax.axis_index("layer")
    queries, tokens, _ = qin.shape
    k_in, k_out = pin.shape[0], pout.shape[0]
    blocks, blk, _ = hess.shape
    rows = store_hbm.shape[0]
    chunks = part.shape[0]
    own = got.shape[2]
    tail = rows - (chunks - 1) * CHUNK

    def load(source, target, index):
        copy = pltpu.make_async_copy(source, target, load_sem.at[index])
        copy.start()
        return copy

    loads = [
        load(qin_hbm.at[0], qin, 0),
        load(pin_hbm.at[0], pin, 1),
        load(qgr_hbm.at[0], qgr, 2),
        load(pout_hbm.at[0], pout, 3),
        load(hess_hbm.at[0], hess, 4),
    ]
    store_loads = []
    for c in range(chunks):
        size = CHUNK if c < chunks - 1 else tail
        at = pl.ds(c * CHUNK, size)
        store_loads.append(load(store_hbm.at[at], store.at[at], 5 + c))

    barrier = pltpu.get_barrier_semaphore()
    for hop in range(1, stores):
        pl.semaphore_signal(
            barrier, inc=1, device_id={"store": lax.rem(my_store + hop, stores)}, device_id_type=MESH
        )
    for hop in range(1, layers):
        pl.semaphore_signal(
            barrier, inc=1, device_id={"layer": lax.rem(my_layer + hop, layers)}, device_id_type=MESH
        )

    depth = expand.shape[0]
    sketch = blocks * blk
    row = lax.rem(lax.broadcasted_iota(jnp.int32, (depth, LANES), 0), LANES)
    col = lax.broadcasted_iota(jnp.int32, (depth, LANES), 1)
    per_block = blk // k_in
    pair = 2 if blocks % 2 == 0 else 1
    step_rows = min(LANES, unit.shape[0])
    steps = unit.shape[0] // step_rows
    for b in range(blocks):
        hit = row == k_in + b * per_block + col // k_in
        expand[:, b * blk : (b + 1) * blk] = jnp.where(hit, 1.0, 0.0).astype(bf16)
    expand[:, sketch:] = jnp.where(row == lax.rem(col, k_in), 1.0, 0.0).astype(bf16)
    store[rows:, :] = jnp.zeros((chunks * CHUNK - rows, store.shape[1]), bf16)
    mixed[...] = jnp.zeros_like(mixed)

    loads[0].wait()
    loads[1].wait()
    mixed[:, 0:k_in] = contract(qin[...].reshape(queries * tokens, -1), pin[...])
    loads[2].wait()
    loads[3].wait()
    mixed[:, k_in : k_in + k_out] = contract(qgr[...].reshape(queries * tokens, -1), pout[...])
    for t in range(tokens):
        value = mixed[pl.ds(t, queries, stride=tokens), :]
        high = value.astype(bf16)
        factors[my_store, t * queries : (t + 1) * queries, 0:LANES] = high

    pl.semaphore_wait(barrier, stores + layers - 2)

    def factor_copy(hop):
        return pltpu.make_async_remote_copy(
            src_ref=factors.at[my_store],
            dst_ref=factors.at[my_store],
            send_sem=fsend_sem.at[hop - 1],
            recv_sem=frecv_sem.at[my_store],
            device_id={"store": lax.rem(my_store + hop, stores)},
            device_id_type=MESH,
        )

    def nearest(k):
        up = k + (my_store <= k).astype(jnp.int32)
        down = stores - 1 - k
        down = down - (down <= my_store).astype(jnp.int32)
        return jnp.where(2 * my_store < stores, up, down)

    def await_factors(source):
        pltpu.make_async_remote_copy(
            src_ref=factors.at[source],
            dst_ref=factors.at[source],
            send_sem=fsend_sem.at[0],
            recv_sem=frecv_sem.at[source],
            device_id={"store": source},
            device_id_type=MESH,
        ).wait_recv()

    def precondition(sources):
        count = len(sources)
        joined = [factors[source] for source in sources]
        joined = joined[0] if count == 1 else jnp.concatenate(joined, axis=0)

        def spread(first, size):
            value = jnp.dot(joined, expand[:, first : first + size], preferred_element_type=f32)
            return value.reshape(count, tokens, queries, size)

        features = spread(sketch, blk)
        total = jnp.zeros((count * queries, blk), f32)
        outers = []
        for b in range(0, blocks, pair):
            wide = spread(b * blk, pair * blk)
            for i in range(pair):
                outer = jnp.sum(wide[..., i * blk : (i + 1) * blk] * features, axis=1)
                outers.append(outer.reshape(count * queries, blk).astype(bf16))
        for b in range(blocks):
            precond = jnp.dot(outers[b], hess[b], preferred_element_type=f32)
            total += precond * precond
            precond = precond.astype(bf16)
            for n, source in enumerate(sources):
                to = pl.ds(pl.multiple_of(source * queries, queries), queries)
                unit[to, b * blk : (b + 1) * blk] = precond[n * queries : (n + 1) * queries]
        square = jnp.broadcast_to(jnp.sum(total, axis=1, keepdims=True), total.shape) * 0.25
        for n, source in enumerate(sources):
            to = pl.ds(pl.multiple_of(source * queries, queries), queries)
            norms[to, :] = square[n * queries : (n + 1) * queries]

    for hop in range(1, stores):
        factor_copy(hop).start()
    loads[4].wait()
    precondition([my_store])

    def arrived(step):
        sources = [nearest(step * group + k) for k in range(group)]
        for source in sources:
            await_factors(source)
        precondition(sources)

    if stores - 1 <= 4:
        for step in range((stores - 1) // group):
            arrived(step)
    else:
        repeat((stores - 1) // group, arrived)

    def part_copy(c, hop):
        peer = lax.rem(my_layer + hop, layers)
        return pltpu.make_async_remote_copy(
            src_ref=part.at[c, pl.ds(pl.multiple_of(peer * own, own), own)],
            dst_ref=got.at[c, hop - 1],
            send_sem=psend_sem.at[c, hop - 1],
            recv_sem=precv_sem.at[c, hop - 1],
            device_id={"layer": peer},
            device_id_type=MESH,
        )

    lane = lax.broadcasted_iota(jnp.int32, (step_rows, CHUNK), 1)
    for c in range(chunks):
        store_loads[c].wait()

        def score(step, c=c):
            to = pl.ds(pl.multiple_of(step * step_rows, step_rows), step_rows)
            value = contract(unit[to, :], store[c * CHUNK : (c + 1) * CHUNK, :])
            if c == chunks - 1:
                norm = norms[to, 0:1]
                high = norm.astype(bf16).astype(f32)
                value = jnp.where(lane == tail, high, value)
                value = jnp.where(lane == tail + 1, norm - high, value)
            part[c, to, :] = value.astype(bf16)

        repeat(steps, score)
        for hop in range(1, layers):
            part_copy(c, hop).start()

    mine = pl.ds(pl.multiple_of(my_layer * own, own), own)
    sums = []
    for c in range(chunks):
        value = part[c, mine, :].astype(f32)
        for hop in range(1, layers):
            part_copy(c, hop).wait_recv()
            value += got[c, hop - 1].astype(f32)
        sums.append(value)
    square = (sums[-1][:, tail : tail + 1] + sums[-1][:, tail + 1 : tail + 2]) * 4.0
    scale = lax.rsqrt(square + epsilon)
    for c in range(chunks):
        size = CHUNK if c < chunks - 1 else tail
        value = jnp.where(scale > 0.0, sums[c] * scale, 0.0).astype(bf16)
        out_ref[:, c * CHUNK : c * CHUNK + size] = value[:, :size]

    for hop in range(1, stores):
        factor_copy(hop).wait_send()
    for c in range(chunks):
        for hop in range(1, layers):
            part_copy(c, hop).wait_send()


def shards(stores, layers, query_inputs, query_grads, proj_in, proj_out, hess_inv, store_sketch):
    _, queries, tokens, width = query_inputs.shape
    k_in, k_out = proj_in.shape[1], proj_out.shape[1]
    _, blocks, blk, _ = hess_inv.shape
    rows, sketch = store_sketch.shape
    chunks = -(-(rows + 2) // CHUNK)
    every = queries * stores
    own = every // layers
    group = GROUP if (stores - 1) % GROUP == 0 else 1
    scratch = [
        pltpu.VMEM((queries, tokens, width), bf16),
        pltpu.VMEM((queries, tokens, width), bf16),
        pltpu.VMEM((k_in, width), bf16),
        pltpu.VMEM((k_out, width), bf16),
        pltpu.VMEM((blocks, blk, blk), bf16),
        pltpu.VMEM((chunks * CHUNK, sketch), bf16),
        pltpu.VMEM((tokens * queries, LANES), f32),
        pltpu.VMEM((stores, tokens * queries, LANES), bf16),
        pltpu.VMEM((LANES, sketch + blk), bf16),
        pltpu.VMEM((every, sketch), bf16),
        pltpu.VMEM((every, LANES), f32),
        pltpu.VMEM((chunks, every, CHUNK), bf16),
        pltpu.VMEM((chunks, layers - 1, own, CHUNK), bf16),
        pltpu.SemaphoreType.DMA((5 + chunks,)),
        pltpu.SemaphoreType.DMA((stores - 1,)),
        pltpu.SemaphoreType.DMA((stores,)),
        pltpu.SemaphoreType.DMA((chunks, layers - 1)),
        pltpu.SemaphoreType.DMA((chunks, layers - 1)),
    ]
    return pl.pallas_call(
        functools.partial(kernel, stores, layers, group),
        out_shape=pltpu.VMEM((own, rows), bf16),
        in_specs=[pl.BlockSpec(memory_space=pltpu.HBM)] * 6,
        out_specs=pl.BlockSpec(memory_space=pltpu.VMEM),
        scratch_shapes=scratch,
        compiler_params=pltpu.CompilerParams(
            collective_id=0, has_side_effects=True, vmem_limit_bytes=48 * 2**20
        ),
    )(
        *(
            pltpu.with_memory_space_constraint(x, pltpu.HBM)
            for x in (query_inputs, query_grads, proj_in, proj_out, hess_inv, store_sketch)
        )
    )


def solution(mesh):
    return jax.shard_map(
        functools.partial(shards, mesh.shape["store"], mesh.shape["layer"]),
        mesh=mesh,
        in_specs=(
            P("layer", ("groups", "store"), None, None),
            P("layer", ("groups", "store"), None, None),
            P("layer", None, None),
            P("layer", None, None),
            P("layer", None, None, None),
            P(("groups", "store"), "layer"),
        ),
        out_specs=P(("groups", "layer"), "store"),
        check_vma=False,
    )
```

```python
import functools

import jax
import jax.numpy as jnp
from jax import lax
from jax.experimental import pallas as pl
from jax.experimental.pallas import tpu as pltpu
from jax.sharding import PartitionSpec as P

epsilon = 1e-06
MESH = pl.DeviceIdType.MESH
CHUNK = 384
GROUP = 1
LANES = 128
f32, bf16 = jnp.float32, jnp.bfloat16


def contract(a, b):
    return lax.dot_general(a, b, (((1,), (1,)), ((), ())), preferred_element_type=f32)


def repeat(count, body):
    if count == 1:
        body(0)
    else:
        lax.fori_loop(0, count, lambda i, _: (body(i), None)[1], None)


def kernel(
    stores, layers, group,
    qin_hbm, qgr_hbm, pin_hbm, pout_hbm, hess_hbm, store_hbm, out_ref,
    qin, qgr, pin, pout, hess, store, mixed, factors, expand, unit, norms, part, got,
    load_sem, fsend_sem, frecv_sem, psend_sem, precv_sem,
):
    my_store, my_layer = lax.axis_index("store"), lax.axis_index("layer")
    queries, tokens, _ = qin.shape
    k_in, k_out = pin.shape[0], pout.shape[0]
    blocks, blk, _ = hess.shape
    rows = store_hbm.shape[0]
    chunks = part.shape[0]
    own = got.shape[2]
    tail = rows - (chunks - 1) * CHUNK

    barrier = pltpu.get_barrier_semaphore()
    for hop in range(1, stores):
        pl.semaphore_signal(
            barrier, inc=1, device_id={"store": lax.rem(my_store + hop, stores)}, device_id_type=MESH
        )
    for hop in range(1, layers):
        pl.semaphore_signal(
            barrier, inc=1, device_id={"layer": lax.rem(my_layer + hop, layers)}, device_id_type=MESH
        )

    def load(source, target, index):
        copy = pltpu.make_async_copy(source, target, load_sem.at[index])
        copy.start()
        return copy

    loads = [
        load(qin_hbm.at[0], qin, 0),
        load(pin_hbm.at[0], pin, 1),
        load(qgr_hbm.at[0], qgr, 2),
        load(pout_hbm.at[0], pout, 3),
        load(hess_hbm.at[0], hess, 4),
    ]
    store_loads = []
    for c in range(chunks):
        size = CHUNK if c < chunks - 1 else tail
        at = pl.ds(c * CHUNK, size)
        store_loads.append(load(store_hbm.at[at], store.at[at], 5 + c))

    depth = expand.shape[0]
    sketch = blocks * blk
    row = lax.rem(lax.broadcasted_iota(jnp.int32, (depth, LANES), 0), LANES)
    col = lax.broadcasted_iota(jnp.int32, (depth, LANES), 1)
    per_block = blk // k_in
    pair = 1
    step_rows = min(LANES, unit.shape[0])
    steps = unit.shape[0] // step_rows
    for b in range(blocks):
        hit = row == k_in + b * per_block + col // k_in
        expand[:, b * blk : (b + 1) * blk] = jnp.where(hit, 1.0, 0.0).astype(bf16)
    expand[:, sketch:] = jnp.where(row == lax.rem(col, k_in), 1.0, 0.0).astype(bf16)
    store[rows:, :] = jnp.zeros((chunks * CHUNK - rows, store.shape[1]), bf16)
    mixed[...] = jnp.zeros_like(mixed)

    loads[0].wait()
    loads[1].wait()
    mixed[:, 0:k_in] = contract(qin[...].reshape(queries * tokens, -1), pin[...])
    loads[2].wait()
    loads[3].wait()
    mixed[:, k_in : k_in + k_out] = contract(qgr[...].reshape(queries * tokens, -1), pout[...])
    for t in range(tokens):
        value = mixed[pl.ds(t, queries, stride=tokens), :]
        high = value.astype(bf16)
        factors[my_store, t * queries : (t + 1) * queries, 0:LANES] = high

    pl.semaphore_wait(barrier, stores + layers - 2)

    def factor_copy(hop):
        return pltpu.make_async_remote_copy(
            src_ref=factors.at[my_store],
            dst_ref=factors.at[my_store],
            send_sem=fsend_sem.at[hop - 1],
            recv_sem=frecv_sem.at[my_store],
            device_id={"store": lax.rem(my_store + hop, stores)},
            device_id_type=MESH,
        )

    def nearest(k):
        up = k + (my_store <= k).astype(jnp.int32)
        down = stores - 1 - k
        down = down - (down <= my_store).astype(jnp.int32)
        return jnp.where(2 * my_store < stores, up, down)

    def await_factors(source):
        pltpu.make_async_remote_copy(
            src_ref=factors.at[source],
            dst_ref=factors.at[source],
            send_sem=fsend_sem.at[0],
            recv_sem=frecv_sem.at[source],
            device_id={"store": source},
            device_id_type=MESH,
        ).wait_recv()

    def precondition(sources):
        count = len(sources)
        joined = [factors[source] for source in sources]
        joined = joined[0] if count == 1 else jnp.concatenate(joined, axis=0)

        def spread(first, size):
            value = jnp.dot(joined, expand[:, first : first + size], preferred_element_type=f32)
            return value.reshape(count, tokens, queries, size)

        features = spread(sketch, blk)
        total = jnp.zeros((count * queries, blk), f32)
        outers = []
        for b in range(0, blocks, pair):
            wide = spread(b * blk, pair * blk)
            for i in range(pair):
                outer = jnp.sum(wide[..., i * blk : (i + 1) * blk] * features, axis=1)
                outers.append(outer.reshape(count * queries, blk).astype(bf16))
        for b in range(blocks):
            precond = jnp.dot(outers[b], hess[b], preferred_element_type=f32)
            total += precond * precond
            precond = precond.astype(bf16)
            for n, source in enumerate(sources):
                to = pl.ds(pl.multiple_of(source * queries, queries), queries)
                unit[to, b * blk : (b + 1) * blk] = precond[n * queries : (n + 1) * queries]
        square = jnp.broadcast_to(jnp.sum(total, axis=1, keepdims=True), total.shape) * 0.25
        for n, source in enumerate(sources):
            to = pl.ds(pl.multiple_of(source * queries, queries), queries)
            norms[to, :] = square[n * queries : (n + 1) * queries]

    for hop in range(1, stores):
        factor_copy(hop).start()
    loads[4].wait()
    precondition([my_store])

    def arrived(step):
        sources = [nearest(step * group + k) for k in range(group)]
        for source in sources:
            await_factors(source)
        precondition(sources)

    if stores - 1 <= 4:
        for step in range((stores - 1) // group):
            arrived(step)
    else:
        repeat((stores - 1) // group, arrived)

    def part_copy(c, hop):
        peer = lax.rem(my_layer + hop, layers)
        return pltpu.make_async_remote_copy(
            src_ref=part.at[c, pl.ds(pl.multiple_of(peer * own, own), own)],
            dst_ref=got.at[c, hop - 1],
            send_sem=psend_sem.at[c, hop - 1],
            recv_sem=precv_sem.at[c, hop - 1],
            device_id={"layer": peer},
            device_id_type=MESH,
        )

    lane = lax.broadcasted_iota(jnp.int32, (step_rows, CHUNK), 1)
    for c in range(chunks):
        store_loads[c].wait()

        def score(step, c=c):
            to = pl.ds(pl.multiple_of(step * step_rows, step_rows), step_rows)
            value = contract(unit[to, :], store[c * CHUNK : (c + 1) * CHUNK, :])
            if c == chunks - 1:
                norm = norms[to, 0:1]
                high = norm.astype(bf16).astype(f32)
                value = jnp.where(lane == tail, high, value)
                value = jnp.where(lane == tail + 1, norm - high, value)
            part[c, to, :] = value.astype(bf16)

        repeat(steps, score)
        for hop in range(1, layers):
            part_copy(c, hop).start()

    mine = pl.ds(pl.multiple_of(my_layer * own, own), own)
    sums = []
    for c in range(chunks):
        value = part[c, mine, :].astype(f32)
        for hop in range(1, layers):
            part_copy(c, hop).wait_recv()
            value += got[c, hop - 1].astype(f32)
        sums.append(value)
    square = (sums[-1][:, tail : tail + 1] + sums[-1][:, tail + 1 : tail + 2]) * 4.0
    scale = lax.rsqrt(square + epsilon)
    for c in range(chunks):
        size = CHUNK if c < chunks - 1 else tail
        value = jnp.where(scale > 0.0, sums[c] * scale, 0.0).astype(bf16)
        out_ref[:, c * CHUNK : c * CHUNK + size] = value[:, :size]

    for hop in range(1, stores):
        factor_copy(hop).wait_send()
    for c in range(chunks):
        for hop in range(1, layers):
            part_copy(c, hop).wait_send()


def shards(stores, layers, query_inputs, query_grads, proj_in, proj_out, hess_inv, store_sketch):
    _, queries, tokens, width = query_inputs.shape
    k_in, k_out = proj_in.shape[1], proj_out.shape[1]
    _, blocks, blk, _ = hess_inv.shape
    rows, sketch = store_sketch.shape
    chunks = -(-(rows + 2) // CHUNK)
    every = queries * stores
    own = every // layers
    group = GROUP if (stores - 1) % GROUP == 0 else 1
    scratch = [
        pltpu.VMEM((queries, tokens, width), bf16),
        pltpu.VMEM((queries, tokens, width), bf16),
        pltpu.VMEM((k_in, width), bf16),
        pltpu.VMEM((k_out, width), bf16),
        pltpu.VMEM((blocks, blk, blk), bf16),
        pltpu.VMEM((chunks * CHUNK, sketch), bf16),
        pltpu.VMEM((tokens * queries, LANES), f32),
        pltpu.VMEM((stores, tokens * queries, LANES), bf16),
        pltpu.VMEM((LANES, sketch + blk), bf16),
        pltpu.VMEM((every, sketch), bf16),
        pltpu.VMEM((every, LANES), f32),
        pltpu.VMEM((chunks, every, CHUNK), bf16),
        pltpu.VMEM((chunks, layers - 1, own, CHUNK), bf16),
        pltpu.SemaphoreType.DMA((5 + chunks,)),
        pltpu.SemaphoreType.DMA((stores - 1,)),
        pltpu.SemaphoreType.DMA((stores,)),
        pltpu.SemaphoreType.DMA((chunks, layers - 1)),
        pltpu.SemaphoreType.DMA((chunks, layers - 1)),
    ]
    return pl.pallas_call(
        functools.partial(kernel, stores, layers, group),
        out_shape=pltpu.VMEM((own, rows), bf16),
        in_specs=[pl.BlockSpec(memory_space=pltpu.HBM)] * 6,
        out_specs=pl.BlockSpec(memory_space=pltpu.VMEM),
        scratch_shapes=scratch,
        compiler_params=pltpu.CompilerParams(
            collective_id=0, has_side_effects=True, vmem_limit_bytes=48 * 2**20
        ),
    )(
        *(
            pltpu.with_memory_space_constraint(x, pltpu.HBM)
            for x in (query_inputs, query_grads, proj_in, proj_out, hess_inv, store_sketch)
        )
    )


def solution(mesh):
    return jax.shard_map(
        functools.partial(shards, mesh.shape["store"], mesh.shape["layer"]),
        mesh=mesh,
        in_specs=(
            P("layer", ("groups", "store"), None, None),
            P("layer", ("groups", "store"), None, None),
            P("layer", None, None),
            P("layer", None, None),
            P("layer", None, None, None),
            P(("groups", "store"), "layer"),
        ),
        out_specs=P(("groups", "layer"), "store"),
        check_vma=False,
    )
```
